128 devices in a mesh: run: 4 (over y), prec: 32 (over x, z, core).
Axes of the slice: x: 4, y: 4, z: 4, core: 2. Of those that a mesh axis runs over, the one named last changes fastest.
Arguments:
- chromatograms: bfloat16 [32, 65536, 256], P('run', 'prec'), may hold values from 0.049804688 to 20
- standards: int32 [32, 11], P('run'), may hold values from 0 to 255, as said below
- library: int32 [11], replicated, may hold values from 0 to 255, as said below
- owner_of: int32 [65536, 1], P('prec'), may hold values from 0 to 31; in each aligned block of 512 rows (0 to 511, 512 to 1023, ...) at most 32 rows name the same one
- local_group: int32 [65536], P('prec'), may hold values from 0 to 511
- quality: bfloat16 [65536], P('prec'), may hold values from 0.25 to 4
Outputs:
- summary: bfloat16 [32, 16384, 256], P('run', 'prec')
The draws below stay inside these ranges and needn't reach their ends.
Inputs may be any that keep to these rules, and one draw needn't show every extreme that they name: library starts at 0, ends at 255 and rises strictly. `standards`: each run's row starts at 0, ends at 255 and rises strictly. `owner_of`: in each aligned block of 512 rows no owner is named more than 32 times.
All inputs are finite; a program needn't handle non-finite values.
Results may differ from the reference program's by a relative error of at most 0.004.
Values may be sent and summed in bfloat16 or wider, within the bound.
A program may use at most 128 MiB of HBM per device.

```python
import math
import jax
import jax.numpy as jnp
import numpy as np
from jax import lax

PTS = 256
RUNS = 32
STANDARDS = 11
GRP_DEV = 512
P_SUB = 512
OWNERS = 32
MOST = 32
PREC = 65536
GROUPS = 16384


def library_points(key):
    spacing = (PTS - 1) // (STANDARDS - 1)
    steps = jnp.arange(STANDARDS, dtype=jnp.int32)
    jitter = jax.random.randint(jax.random.fold_in(key, 11), (STANDARDS,), 0, spacing // 2 + 1)
    points = steps * spacing + jitter
    points = points.at[0].set(0).at[STANDARDS - 1].set(PTS - 1)
    return points.astype(jnp.int32)


def draw_library(key, part):
    return library_points(key)


def draw_standards(key, part):
    spacing = (PTS - 1) // (STANDARDS - 1)
    points = library_points(key)
    offsets = jax.random.randint(jax.random.fold_in(key, 23), (RUNS, STANDARDS), -(spacing // 4), spacing // 4 + 1)
    observed = jnp.clip(points[None, :] + offsets, 0, PTS - 1)
    observed = observed.at[:, 0].set(0).at[:, STANDARDS - 1].set(PTS - 1)
    return observed.astype(jnp.int32)


def set_ends(drawn, rng, least, top_value):
    shape = drawn.shape
    index_at = [jax.random.randint(jax.random.fold_in(rng, axis), (), 0, shape[axis]) for axis in range(len(shape))]
    drawn = drawn.at[tuple(index_at)].set(least)
    longest = shape.index(max(shape))
    index_at[longest] = (index_at[longest] + 1) % shape[longest]
    return drawn.at[tuple(index_at)].set(top_value)


def levels(key, shape, cuts, smallest, top_value):
    gain = 1.0
    for dim, parts in cuts:
        heights = jax.random.uniform(jax.random.fold_in(jax.random.fold_in(key, 6), dim), (parts,), jnp.float32, smallest / len(cuts), top_value / len(cuts))
        gain = gain * jnp.repeat(jnp.exp(heights), shape[dim] // parts).reshape((-1,) + (1,) * (len(shape) - 1 - dim))
    return gain


def deal_out(key, own, number, rows, number_of, top, bound, lean):
    sequence = jax.random.permutation(key, number_of)
    packed, ordinary = shares(number_of, rows * top, bound, lean, True), shares(number_of, rows * top, bound, lean, False)
    places = jnp.arange(number_of)

    def named(sizes, rotation):
        used = int((sizes > 0).sum())
        fixed = max(1, used // 4)
        shifted = fixed + (places - fixed + rotation * (used - fixed)) % max(1, number_of - fixed)
        return jnp.zeros((number_of,), jnp.int32).at[sequence[jnp.where(places < fixed, places, shifted)]].set(jnp.asarray(sizes, jnp.int32))

    sizes = jnp.where(number % 4 == 0, named(packed, number // 4), named(ordinary, number - number // 4 - 1))
    mixed = jax.random.permutation(jax.random.fold_in(own, 3), number_of)
    donor, taker = mixed[0:number_of // 2 * 2:2], mixed[1:number_of // 2 * 2:2]
    room = jnp.minimum(sizes[donor] - 1, bound - sizes[taker]) // 2
    room = jnp.where((donor == sequence[0]) | (taker == sequence[0]) | (sizes[taker] == 0), 0, jnp.maximum(room, 0))
    shifted = jax.random.randint(jax.random.fold_in(own, 4), (number_of // 2,), 0, 1 << 20) % (room + 1)
    sizes = sizes.at[donor].add(-shifted).at[taker].add(shifted)
    members = jnp.searchsorted(jnp.cumsum(sizes), jnp.arange(rows * top), side="right").astype(jnp.int32)
    table = members.reshape(top, rows).T
    table = table[jax.random.permutation(jax.random.fold_in(own, 1), rows)]
    rotation = jax.random.randint(jax.random.fold_in(own, 2), (rows, 1), 0, top)
    return jnp.take_along_axis(table, (jnp.arange(top)[None, :] + rotation) % top, axis=1)


def shares(count, total, limit, lean, full):
    loads = [(1 << 20) // math.isqrt(grade ** lean) + 1 for grade in range(1, count + 1)]
    largest = limit if full else min(limit, max(-(-total // count), total * loads[0] // sum(loads)))
    least = 1 if total - largest >= count - 1 else 0
    given, rest = [largest] + [least] * (count - 1), total - largest - least * (count - 1)
    while rest > 0:
        free = [i for i in range(1, count) if given[i] < largest] or [i for i in range(1, count) if given[i] < limit]
        whole, left = sum([loads[i] for i in free]), rest
        for i in free:
            addition = min(limit - given[i], max(1, left * loads[i] // whole), rest)
            given[i] = given[i] + addition
            rest = rest - addition
    return np.array(given)


def setup_inputs(seed: int = 0) -> dict:
    splits = jax.random.split(jax.random.key(seed), 7)
    chromatograms = jnp.clip(jnp.exp(math.log(20.0) - 5.9953784 * jax.random.uniform(splits[0], (RUNS, PREC, PTS), jnp.float32) ** levels(splits[0], (RUNS, PREC, PTS), ((0, 4), (1, 32)), -0.2, 0.2)), 0.049804688, 20.0).astype(jnp.bfloat16)
    standards = draw_standards(jax.random.fold_in(splits[6], 71), 0)
    library = draw_library(jax.random.fold_in(splits[6], 71), 0)
    owner_of_keys = jax.random.split(jax.random.fold_in(splits[3], 1), PREC // P_SUB)
    owner_of_turns = jax.random.permutation(jax.random.fold_in(splits[3], 3), PREC // P_SUB)
    owner_of = jax.vmap(lambda own, number: deal_out(jax.random.fold_in(splits[3], 2), own, number, P_SUB, OWNERS, 1, MOST, 2))(owner_of_keys, owner_of_turns).reshape((PREC, 1))
    local_group = set_ends(jax.random.randint(splits[4], (PREC,), 0, GRP_DEV), jax.random.fold_in(splits[4], 1), 0, GRP_DEV - 1).astype(jnp.int32)
    quality = jnp.clip(jnp.exp(math.log(4.0) - 2.7725887 * jax.random.uniform(splits[5], (PREC,), jnp.float32) ** levels(splits[5], (PREC,), ((0, 32),), -0.2, 0.2)), 0.25, 4.0).astype(jnp.bfloat16)
    return dict(chromatograms=chromatograms, standards=standards, library=library, owner_of=owner_of, local_group=local_group, quality=quality)


def source_points(standards, library, width):
    count = library.shape[0]
    points = jnp.arange(width, dtype=jnp.int32)
    t_float = points.astype(jnp.float32)
    segment = jnp.sum((library[1:count - 1][None, :] <= points[:, None]).astype(jnp.int32), axis=1)
    pick = (segment[:, None] == jnp.arange(count - 1, dtype=jnp.int32)[None, :]).astype(jnp.float32)
    lib_f = library.astype(jnp.float32)
    obs_f = standards.astype(jnp.float32)
    slope = (obs_f[:, 1:] - obs_f[:, :-1]) / (lib_f[1:] - lib_f[:-1])[None, :]
    mapped = obs_f[:, None, :-1] + (t_float[None, :, None] - lib_f[None, None, :-1]) * slope[:, None, :]
    return jnp.sum(mapped * pick[None], axis=2)


def reference(chromatograms, standards, library, owner_of, local_group, quality):
    source = source_points(standards, library, PTS)
    group = owner_of[:, 0] * GRP_DEV + local_group
    weight = quality.astype(jnp.float32)

    def one_run(pair):
        values, src = pair
        low = jnp.floor(src)
        low_index = low.astype(jnp.int32)
        high_index = jnp.minimum(low_index + 1, PTS - 1)
        w_low = (1.0 - (src - low)).astype(jnp.bfloat16)
        w_high = (1.0 - (low + 1.0 - src)).astype(jnp.bfloat16)
        w_low, w_high = lax.optimization_barrier((w_low, w_high))
        w_low = w_low.astype(jnp.float32)
        w_high = w_high.astype(jnp.float32)
        lower = jnp.take(values, low_index, axis=1).astype(jnp.float32)
        upper = jnp.take(values, high_index, axis=1).astype(jnp.float32)
        resampled = lower * w_low[None, :] + upper * w_high[None, :]
        contribution = (weight[:, None] * jnp.log1p(resampled)).astype(jnp.bfloat16)
        return jax.ops.segment_sum(contribution.astype(jnp.float32), group, num_segments=GROUPS)

    totals = lax.map(one_run, (chromatograms, source))
    return (0.25 * totals).astype(jnp.bfloat16)
```

```python
import jax
import jax.numpy as jnp
from jax import lax
from jax.experimental import pallas as pl
from jax.experimental.pallas import tpu as pltpu
from jax.sharding import PartitionSpec as P

MESH = pl.DeviceIdType.MESH
F32 = jnp.float32
BF16 = jnp.bfloat16
RUNS = 8
BLOCKS = 4
BLOCK = 512
MOST = 32
OWNERS = 32
GRP = 512
PTS = 256
STANDARDS = 11
SIDE = 4
LINE = 8
SLOTS = 4


def nt_dot(a, b):
    return lax.dot_general(a, b, (((1,), (1,)), ((), ())), preferred_element_type=F32)


def kernel(
    x_hbm, std, lib, own, lg, q, out,
    xbuf, perm, tri, qcol, srcs, tags, rtags, member, sbuf, rbuf, dbuf, ddbuf, mine,
    x_sem, tag_ssem, tag_rsem, s_sem, r_sem, d_sem, dd_sem,
):
    yy = lax.axis_index("run")
    pp = lax.axis_index("prec")
    xx, zz, cc = pp // 8, (pp // 2) % 4, pp % 2

    def along(order, first, second, core):
        gx = (1 - order) * first + order * second
        gz = (1 - order) * second + order * first
        return gx * 8 + gz * 2 + core

    def load(j):
        return pltpu.make_async_copy(x_hbm.at[j], xbuf.at[j % 2], x_sem.at[j % 2])

    barrier = pltpu.get_barrier_semaphore()
    for order in range(2):
        first = (xx, zz)[order]
        second = (zz, xx)[order]
        for df in range(SIDE):
            for dc in range(2):
                if (df, dc) == (0, 0) or (order == 1 and df == 0):
                    continue
                other = along(order, (first + df) % SIDE, second, (cc + dc) % 2)
                pl.semaphore_signal(barrier, inc=1, device_id=(yy, other), device_id_type=MESH)
    load(0).start()
    load(1).start()

    t = lax.broadcasted_iota(jnp.int32, (1, PTS), 1)
    later = [lib[k] <= t for k in range(1, STANDARDS - 1)]

    def pick(values):
        got = jnp.full((1, PTS), values[0], jnp.int32)
        for mask, value in zip(later, values[1:]):
            got = jnp.where(mask, value, got)
        return got.astype(F32)

    lib_at = pick([lib[k] for k in range(STANDARDS - 1)])
    lib_gap = pick([lib[k + 1] - lib[k] for k in range(STANDARDS - 1)])
    for r in range(RUNS):
        base = pick([std[r, k] for k in range(STANDARDS - 1)])
        gap = pick([std[r, k + 1] - std[r, k] for k in range(STANDARDS - 1)])
        srcs[r] = base + (t.astype(F32) - lib_at) * (gap / lib_gap)

    tri[...] = (
        lax.broadcasted_iota(jnp.int32, (BLOCK, BLOCK), 0) < lax.broadcasted_iota(jnp.int32, (BLOCK, BLOCK), 1)
    ).astype(F32).astype(BF16)
    row = lax.broadcasted_iota(jnp.int32, (64, 1), 0)
    line, inner = row // 8, row % 8
    owner_xz = jnp.where(inner < SIDE, (line // 2) * 8 + inner * 2 + line % 2, -1)
    owner_zx = jnp.where(inner < SIDE, inner * 8 + (line // 2) * 2 + line % 2, -1)
    tag_sum = jnp.zeros((256, 128), F32)
    for b in range(BLOCKS):
        owner = own[b : b + 1, :]
        hit = (owner == lax.broadcasted_iota(jnp.int32, (OWNERS, BLOCK), 0)).astype(F32)
        before = jnp.dot(hit.astype(BF16), tri[...], preferred_element_type=F32)
        rank = jnp.sum(before * hit, axis=0, keepdims=True).astype(jnp.int32)
        place = owner * MOST + rank

        def fill(i, _):
            at = lax.broadcasted_iota(jnp.int32, (256, BLOCK), 0) + i * 256
            perm[b, pl.ds(pl.multiple_of(i * 256, 256), 256), :] = (at == place).astype(F32).astype(BF16)
            return 0

        lax.fori_loop(0, OWNERS * MOST // 256, fill, 0)
        tag = lg[b : b + 1, :] + 1
        low = (tag % 256).astype(F32)
        high = (tag // 256).astype(F32)
        parts = []
        for chosen in (owner_xz, owner_zx):
            mask = chosen == owner
            parts += [jnp.where(mask, low, 0.0), jnp.where(mask, high, 0.0)]
        lane = lax.broadcasted_iota(jnp.int32, (128, BLOCK), 0) - b * MOST
        at_slot = (lane == rank).astype(F32).astype(BF16)
        tag_sum = tag_sum + nt_dot(jnp.concatenate(parts, axis=0).astype(BF16), at_slot)
        qcol[b] = jnp.transpose(jnp.broadcast_to(q[b : b + 1, :], (128, BLOCK)))
    for order in range(2):
        both = tag_sum[order * 128 : order * 128 + 128]
        tags[order] = (both[:64] + 256.0 * both[64:]).reshape(LINE, 8, 128)

    pl.semaphore_wait(barrier, 13)
    for order in range(2):
        first = (xx, zz)[order]
        second = (zz, xx)[order]
        me = first * 2 + cc
        for df in range(SIDE):
            for dc in range(2):
                f2, c2 = (first + df) % SIDE, (cc + dc) % 2
                src, dst = tags.at[order, f2 * 2 + c2], rtags.at[order, me]
                if (df, dc) == (0, 0):
                    pltpu.make_async_copy(src, dst, tag_rsem.at[order]).start()
                else:
                    pltpu.make_async_remote_copy(
                        src_ref=src, dst_ref=dst, send_sem=tag_ssem.at[order], recv_sem=tag_rsem.at[order],
                        device_id=(yy, along(order, f2, second, c2)), device_id_type=MESH,
                    ).start()

    def send_profiles(j):
        order = j % 2
        first = (1 - order) * xx + order * zz
        second = (1 - order) * zz + order * xx
        me = first * 2 + cc
        slot = j % SLOTS
        load(j).wait()
        down = lax.broadcasted_iota(jnp.int32, (PTS, PTS), 0).astype(F32)
        warp = jnp.maximum(0.0, 1.0 - jnp.abs(srcs[j] - down)).astype(BF16)

        def block(b, _):
            rows = pl.ds(pl.multiple_of(b * BLOCK, BLOCK), BLOCK)
            seen = jnp.dot(xbuf[j % 2, rows, :], warp, preferred_element_type=F32)
            weight = qcol[b]
            logs = jnp.log(1.0 + seen)
            prof = jnp.concatenate([logs[:, :128] * weight, logs[:, 128:] * weight], axis=1).astype(BF16)
            for half in range(2):
                got = jnp.dot(perm[b, half * 512 : half * 512 + 512, :], prof, preferred_element_type=F32).astype(BF16)
                for i in range(16):
                    o = half * 16 + i
                    ox, oz, oc = o // 8, (o // 2) % 4, o % 2
                    of = (1 - order) * ox + order * oz
                    os = (1 - order) * oz + order * ox
                    sbuf[slot, b, of * 2 + oc, os] = got[i * MOST : (i + 1) * MOST]
            for df in (2, 1, 3, 0):
                for dc in (1, 0):
                    f2, c2 = (first + df) % SIDE, (cc + dc) % 2
                    src, dst = sbuf.at[slot, b, f2 * 2 + c2], rbuf.at[j, me, b]
                    if (df, dc) == (0, 0):
                        pltpu.make_async_copy(src, dst, r_sem.at[j]).start()
                    else:
                        pltpu.make_async_remote_copy(
                            src_ref=src, dst_ref=dst, send_sem=s_sem.at[slot], recv_sem=r_sem.at[j],
                            device_id=(yy, along(order, f2, second, c2)), device_id_type=MESH,
                        ).start()
            return 0

        lax.fori_loop(0, BLOCKS, block, 0)

    def wait_sent(slot):
        some = sbuf.at[slot, :, 0 : LINE - 1]
        pltpu.make_async_copy(some, some, s_sem.at[slot]).wait()

    def members():
        for order in range(2):
            pltpu.make_async_copy(rtags.at[order], rtags.at[order], tag_rsem.at[order]).wait()
            some = tags.at[order, 0 : LINE - 1]
            pltpu.make_async_copy(some, some, tag_ssem.at[order]).wait()

            def fill(src, _):
                got = rtags[order, src]
                group = lax.broadcasted_iota(jnp.int32, (GRP, 128), 0).astype(F32) + 1.0
                cols = pl.ds(pl.multiple_of(src * 128, 128), 128)
                for s in range(SIDE):
                    member[order, s, :, cols] = (group == got[s : s + 1]).astype(F32).astype(BF16)
                return 0

            lax.fori_loop(0, LINE, fill, 0)

    def send_sums(j):
        order = j % 2
        first = (1 - order) * xx + order * zz
        second = (1 - order) * zz + order * xx
        slot = j % SLOTS
        pltpu.make_async_copy(rbuf.at[j], rbuf.at[j], r_sem.at[j]).wait()

        def total(s):
            rows = rbuf[j, :, :, s].reshape(LINE * BLOCKS * MOST, PTS)
            return jnp.dot(member[order, s], rows, preferred_element_type=F32)

        def other(i, _):
            k = (i + 1) % 3 + 1
            s = (second + k) % SIDE
            dbuf[slot, k - 1] = total(s).astype(BF16)
            pltpu.make_async_remote_copy(
                src_ref=dbuf.at[slot, k - 1], dst_ref=ddbuf.at[j, k - 1], send_sem=d_sem.at[slot], recv_sem=dd_sem.at[j],
                device_id=(yy, along(order, first, s, cc)), device_id_type=MESH,
            ).start()
            return 0

        lax.fori_loop(0, SIDE - 1, other, 0)
        mine[slot] = total(second)

    def wait_sums(slot):
        pltpu.make_async_copy(dbuf.at[slot], dbuf.at[slot], d_sem.at[slot]).wait()

    def finish(j):
        pltpu.make_async_copy(ddbuf.at[j], ddbuf.at[j], dd_sem.at[j]).wait()
        whole = mine[j % SLOTS]
        for k in range(SIDE - 1):
            whole = whole + ddbuf[j, k].astype(F32)
        out[j] = (0.25 * whole).astype(BF16)

    def step(j, _):
        @pl.when(j < RUNS)
        def _():
            @pl.when(j >= SLOTS)
            def _():
                wait_sent(j % SLOTS)

            send_profiles(j)

            @pl.when(j + 2 < RUNS)
            def _():
                load(j + 2).start()

        @pl.when(j == 1)
        def _():
            members()

        @pl.when((j >= 2) & (j < RUNS + 2))
        def _():
            @pl.when(j - 2 >= SLOTS)
            def _():
                wait_sums((j - 2) % SLOTS)

            send_sums(j - 2)

        @pl.when(j >= 4)
        def _():
            finish(j - 4)

        return 0

    lax.fori_loop(0, RUNS + 4, step, 0)
    for slot in range(SLOTS):
        wait_sent(slot)
        wait_sums(slot)


def per_device(chromatograms, standards, library, owner_of, local_group, quality):
    vmem = pl.BlockSpec(memory_space=pltpu.VMEM)
    smem = pl.BlockSpec(memory_space=pltpu.SMEM)
    return pl.pallas_call(
        kernel,
        out_shape=jax.ShapeDtypeStruct((RUNS, GRP, PTS), BF16),
        in_specs=[pl.BlockSpec(memory_space=pl.ANY), smem, smem, vmem, vmem, vmem],
        out_specs=vmem,
        scratch_shapes=[
            pltpu.VMEM((2, BLOCKS * BLOCK, PTS), BF16),
            pltpu.VMEM((BLOCKS, OWNERS * MOST, BLOCK), BF16),
            pltpu.VMEM((BLOCK, BLOCK), BF16),
            pltpu.VMEM((BLOCKS, BLOCK, 128), F32),
            pltpu.VMEM((RUNS, 1, PTS), F32),
            pltpu.VMEM((2, LINE, 8, 128), F32),
            pltpu.VMEM((2, LINE, 8, 128), F32),
            pltpu.VMEM((2, SIDE, GRP, LINE * BLOCKS * MOST), BF16),
            pltpu.VMEM((SLOTS, BLOCKS, LINE, SIDE, MOST, PTS), BF16),
            pltpu.VMEM((RUNS, LINE, BLOCKS, SIDE, MOST, PTS), BF16),
            pltpu.VMEM((SLOTS, SIDE - 1, GRP, PTS), BF16),
            pltpu.VMEM((RUNS, SIDE - 1, GRP, PTS), BF16),
            pltpu.VMEM((SLOTS, GRP, PTS), F32),
            pltpu.SemaphoreType.DMA((2,)),
            pltpu.SemaphoreType.DMA((2,)),
            pltpu.SemaphoreType.DMA((2,)),
            pltpu.SemaphoreType.DMA((SLOTS,)),
            pltpu.SemaphoreType.DMA((RUNS,)),
            pltpu.SemaphoreType.DMA((SLOTS,)),
            pltpu.SemaphoreType.DMA((RUNS,)),
        ],
        compiler_params=pltpu.CompilerParams(
            collective_id=0, has_side_effects=True, vmem_limit_bytes=62 * 2**20
        ),
    )(
        chromatograms,
        standards,
        library,
        owner_of.reshape(BLOCKS, BLOCK),
        local_group.reshape(BLOCKS, BLOCK),
        quality.astype(F32).reshape(BLOCKS, BLOCK),
    )


def solution(mesh):
    placed = (P("run", "prec", None), P("run", None), P(), P("prec", None), P("prec"), P("prec"))
    return jax.shard_map(
        per_device, mesh=mesh, in_specs=placed, out_specs=P("run", "prec", None), check_vma=False
    )
```

```python
import jax
import jax.numpy as jnp
from jax import lax
from jax.experimental import pallas as pl
from jax.experimental.pallas import tpu as pltpu
from jax.sharding import PartitionSpec as P

MESH = pl.DeviceIdType.MESH
F32 = jnp.float32
BF16 = jnp.bfloat16
RUNS = 8
BLOCKS = 4
BLOCK = 512
MOST = 32
OWNERS = 32
GRP = 512
PTS = 256
STANDARDS = 11
SIDE = 4
SLOTS = 4

LEAVES = (
    ((1, 0), ((2, 3), (3, 0), (3, 1))),
    ((0, 1), ((1, 0), (2, 0), (3, 2))),
    ((0, 3), ((0, 2), (1, 2), (2, 2))),
    ((3, 0), ((1, 3),)),
)
INNER = (((2, 1), (3, 0), 0), ((3, 3), (1, 0), 0), ((1, 1), (3, 0), 1), ((0, 3), (0, 1), 1), ((0, 1), (0, 3), 2))
ROOT = (0, 0)
NODES = tuple(n for n, _, _ in INNER) + (ROOT,)
SELF = 2 * sum(len(ps) for _, ps in LEAVES)


def layout():
    place, feeds, base = {}, {n: [n] for n in NODES}, 0
    for (sx, sz), ps in LEAVES:
        for i, (px, pz) in enumerate(ps):
            place[px, pz] = (base + i, len(ps))
            feeds[(px + sx) % SIDE, (pz + sz) % SIDE].append((px, pz))
        base += 2 * len(ps)
    for i, n in enumerate(NODES):
        place[n] = (base + i, len(NODES))
    return place, feeds


PLACE, FEEDS = layout()
CHUNKS = {n: [PLACE[p][0] + core * PLACE[p][1] for p in FEEDS[n] for core in range(2)] for n in NODES}
ORDER = [chunk for n in NODES for chunk in CHUNKS[n]]
COLUMN = {n: 128 * sum(len(CHUNKS[m]) for m in NODES[:i]) for i, n in enumerate(NODES)}


def nt_dot(a, b):
    return lax.dot_general(a, b, (((1,), (1,)), ((), ())), preferred_element_type=F32)


def to_bf16(mask):
    return mask.astype(F32).astype(BF16)


def kernel(
    x_hbm, std, lib, own, lg, q, out,
    xbuf, perm, tri, qall, qcol, srcs, tags, rtags, member, sbuf, rbuf, dbuf, ddbuf,
    x_sem, tag_ssem, tag_rsem, s_sem, r_sem, d_sem, dd_sem,
):
    yy = lax.axis_index("run")
    pp = lax.axis_index("prec")
    xx, zz, cc = pp // 8, (pp // 2) % 4, pp % 2

    def device(step, core):
        return (yy, ((xx + step[0]) % SIDE) * 8 + ((zz + step[1]) % SIDE) * 2 + core)

    def load(j):
        return pltpu.make_async_copy(x_hbm.at[j], xbuf.at[j % 2], x_sem.at[j % 2])

    barrier = pltpu.get_barrier_semaphore()
    for step, _ in LEAVES:
        for core in range(2):
            pl.semaphore_signal(barrier, inc=1, device_id=device(step, core), device_id_type=MESH)
    pl.semaphore_signal(barrier, inc=1, device_id=device(ROOT, 1 - cc), device_id_type=MESH)
    load(0).start()
    load(1).start()

    t = lax.broadcasted_iota(jnp.int32, (1, PTS), 1)
    later = [lib[k] <= t for k in range(1, STANDARDS - 1)]

    def pick(values):
        got = jnp.full((1, PTS), values[0], jnp.int32)
        for mask, value in zip(later, values[1:]):
            got = jnp.where(mask, value, got)
        return got.astype(F32)

    lib_at = pick([lib[k] for k in range(STANDARDS - 1)])
    lib_gap = pick([lib[k + 1] - lib[k] for k in range(STANDARDS - 1)])
    for r in range(RUNS):
        base = pick([std[r, k] for k in range(STANDARDS - 1)])
        gap = pick([std[r, k + 1] - std[r, k] for k in range(STANDARDS - 1)])
        srcs[r] = base + (t.astype(F32) - lib_at) * (gap / lib_gap)
    tri[...] = to_bf16(
        lax.broadcasted_iota(jnp.int32, (BLOCK, BLOCK), 0) < lax.broadcasted_iota(jnp.int32, (BLOCK, BLOCK), 1)
    )
    qall[...] = q[...].astype(F32)
    tags[...] = jnp.zeros_like(tags)

    def place_block(b):
        def lanes(ref):
            return jnp.concatenate([ref[pl.ds(b * 4 + i, 1), :] for i in range(4)], axis=1)

        owner = lanes(own)
        px = (xx + SIDE - owner // 8) % SIDE
        pz = (zz + SIDE - (owner // 2) % 4) % SIDE
        core = owner % 2
        chunk = jnp.zeros_like(owner)
        for (kx, kz), (start, apart) in PLACE.items():
            chunk = jnp.where((px == kx) & (pz == kz), start + core * apart, chunk)
        hit = (chunk == lax.broadcasted_iota(jnp.int32, (OWNERS, BLOCK), 0)).astype(F32)
        before = jnp.dot(hit.astype(BF16), tri[...], preferred_element_type=F32)
        rank = jnp.sum(before * hit, axis=0, keepdims=True).astype(jnp.int32)
        place = chunk * MOST + rank
        for i in range(4):
            at = lax.broadcasted_iota(jnp.int32, (256, BLOCK), 0) + i * 256
            perm[b, i * 256 : i * 256 + 256, :] = to_bf16(at == place)
        tag = lanes(lg) + 1
        low = hit * (tag % 256).astype(F32)
        high = hit * (tag // 256).astype(F32)
        at_slot = to_bf16(lax.broadcasted_iota(jnp.int32, (128, BLOCK), 0) - b * MOST == rank)
        both = nt_dot(jnp.concatenate([low, high], axis=0).astype(BF16), at_slot)
        tags[...] += jnp.broadcast_to((both[:OWNERS] + 256.0 * both[OWNERS:])[:, None, :], tags.shape)
        for i in range(4):
            weights = qall[pl.ds(b * 4 + i, 1), :]
            qcol[b, i * 128 : i * 128 + 128, :] = jnp.transpose(jnp.broadcast_to(weights, (128, 128)))

    def send_chunks(source, target, send_sem, recv_sem):
        base = 0
        for step, ps in LEAVES:
            n = len(ps)
            for core in range(2):
                pltpu.make_async_remote_copy(
                    src_ref=source.at[pl.ds(base + core * n, n)], dst_ref=target.at[pl.ds(base + cc * n, n)],
                    send_sem=send_sem, recv_sem=recv_sem, device_id=device(step, core), device_id_type=MESH,
                ).start()
            base += 2 * n
        n = len(NODES)
        mine, other = pl.ds(SELF + cc * n, n), pl.ds(SELF + (1 - cc) * n, n)
        pltpu.make_async_remote_copy(
            src_ref=source.at[other], dst_ref=target.at[mine],
            send_sem=send_sem, recv_sem=recv_sem, device_id=device(ROOT, 1 - cc), device_id_type=MESH,
        ).start()
        pltpu.make_async_copy(source.at[mine], target.at[mine], recv_sem).start()

    def wait_bytes(ref, sem):
        pltpu.make_async_copy(ref, ref, sem).wait()

    def send_profiles(j):
        slot = j % SLOTS
        load(j).wait()
        down = lax.broadcasted_iota(jnp.int32, (PTS, PTS), 0).astype(F32)
        warp = jnp.maximum(0.0, 1.0 - jnp.abs(srcs[j] - down)).astype(BF16)

        def block(b, _):
            @pl.when(j == 0)
            def _():
                place_block(b)

            rows = pl.ds(pl.multiple_of(b * BLOCK, BLOCK), BLOCK)
            seen = jnp.dot(xbuf[j % 2, rows, :], warp, preferred_element_type=F32)
            weight = qcol[b]
            logs = jnp.log(1.0 + seen)
            prof = jnp.concatenate([logs[:, :128] * weight, logs[:, 128:] * weight], axis=1).astype(BF16)
            for half in range(2):
                got = jnp.dot(perm[b, half * 512 : half * 512 + 512, :], prof, preferred_element_type=F32)
                sbuf[slot, b, half * 16 : half * 16 + 16] = got.astype(BF16).reshape(16, MOST, PTS)

            @pl.when((j == 0) & (b == 0))
            def _():
                pl.semaphore_wait(barrier, 9)

            send_chunks(sbuf.at[slot, b], rbuf.at[j, b], s_sem.at[slot], r_sem.at[j])
            return 0

        lax.fori_loop(0, BLOCKS, block, 0)

    def wait_sent(slot):
        wait_bytes(sbuf.at[slot, :, 0 : SELF + len(NODES)], s_sem.at[slot])

    def members():
        wait_bytes(rtags, tag_rsem)
        wait_bytes(tags.at[0 : SELF + len(NODES)], tag_ssem)
        group = lax.broadcasted_iota(jnp.int32, (GRP, 128), 0).astype(F32) + 1.0
        for i, chunk in enumerate(ORDER):
            member[:, i * 128 : i * 128 + 128] = to_bf16(group == rtags[chunk, 0:1, :])

    def total(j, node):
        rows = jnp.concatenate([rbuf[j, :, chunk].reshape(BLOCKS * MOST, PTS) for chunk in CHUNKS[node]], axis=0)
        columns = member[:, COLUMN[node] : COLUMN[node] + 128 * len(CHUNKS[node])]
        return jnp.dot(columns, rows, preferred_element_type=F32)

    def children(node):
        return [
            i for i, ((nx, nz), (sx, sz), _) in enumerate(INNER) if ((nx + sx) % SIDE, (nz + sz) % SIDE) == node
        ]

    def of_level(level):
        return [i for i, (_, _, at) in enumerate(INNER) if at == level]

    def sums_of(buffer, slot, level):
        these = of_level(level)
        return buffer.at[slot, these[0] : these[-1] + 1]

    def send_sums(j, level):
        slot = j % SLOTS
        if level == 0:
            wait_bytes(rbuf.at[j], r_sem.at[j])
        else:
            wait_bytes(sums_of(ddbuf, j, level - 1), dd_sem.at[level - 1, j])

        @pl.when(j >= SLOTS)
        def _():
            wait_bytes(sums_of(dbuf, slot, level), d_sem.at[level, slot])

        for i in of_level(level):
            node, step, _ = INNER[i]
            whole = total(j, node)
            for child in children(node):
                whole = whole + ddbuf[j, child].astype(F32)
            dbuf[slot, i] = whole.astype(BF16)
            pltpu.make_async_remote_copy(
                src_ref=dbuf.at[slot, i], dst_ref=ddbuf.at[j, i], send_sem=d_sem.at[level, slot],
                recv_sem=dd_sem.at[level, j], device_id=device(step, cc), device_id_type=MESH,
            ).start()

    def finish(j):
        wait_bytes(sums_of(ddbuf, j, 2), dd_sem.at[2, j])
        whole = total(j, ROOT)
        for child in children(ROOT):
            whole = whole + ddbuf[j, child].astype(F32)
        out[j] = (0.25 * whole).astype(BF16)

    def step(j, _):
        @pl.when(j < RUNS)
        def _():
            @pl.when(j >= SLOTS)
            def _():
                wait_sent(j % SLOTS)

            send_profiles(j)

            @pl.when(j + 2 < RUNS)
            def _():
                load(j + 2).start()

        @pl.when(j == 0)
        def _():
            send_chunks(tags, rtags, tag_ssem, tag_rsem)

        @pl.when(j == LAG - 1)
        def _():
            members()

        for level in range(3):
            @pl.when((j >= level + LAG) & (j < RUNS + level + LAG))
            def _(level=level):
                send_sums(j - level - LAG, level)

        @pl.when(j >= 3 + LAG)
        def _():
            finish(j - 3 - LAG)

        return 0

    lax.fori_loop(0, RUNS + 3 + LAG, step, 0)
    for slot in range(SLOTS):
        wait_sent(slot)
        for level in range(3):
            wait_bytes(sums_of(dbuf, slot, level), d_sem.at[level, slot])


LAG = 1


def per_device(chromatograms, standards, library, owner_of, local_group, quality):
    vmem = pl.BlockSpec(memory_space=pltpu.VMEM)
    smem = pl.BlockSpec(memory_space=pltpu.SMEM)
    chunk = (OWNERS, MOST, PTS)
    return pl.pallas_call(
        kernel,
        out_shape=jax.ShapeDtypeStruct((RUNS, GRP, PTS), BF16),
        in_specs=[pl.BlockSpec(memory_space=pl.ANY), smem, smem, vmem, vmem, vmem],
        out_specs=vmem,
        scratch_shapes=[
            pltpu.VMEM((2, BLOCKS * BLOCK, PTS), BF16),
            pltpu.VMEM((BLOCKS, OWNERS * MOST, BLOCK), BF16),
            pltpu.VMEM((BLOCK, BLOCK), BF16),
            pltpu.VMEM((16, 128), F32),
            pltpu.VMEM((BLOCKS, BLOCK, 128), F32),
            pltpu.VMEM((RUNS, 1, PTS), F32),
            pltpu.VMEM((OWNERS, 8, 128), F32),
            pltpu.VMEM((OWNERS, 8, 128), F32),
            pltpu.VMEM((GRP, OWNERS * 128), BF16),
            pltpu.VMEM((SLOTS, BLOCKS, *chunk), BF16),
            pltpu.VMEM((RUNS, BLOCKS, *chunk), BF16),
            pltpu.VMEM((SLOTS, len(INNER), GRP, PTS), BF16),
            pltpu.VMEM((RUNS, len(INNER), GRP, PTS), BF16),
            pltpu.SemaphoreType.DMA((2,)),
            pltpu.SemaphoreType.DMA,
            pltpu.SemaphoreType.DMA,
            pltpu.SemaphoreType.DMA((SLOTS,)),
            pltpu.SemaphoreType.DMA((RUNS,)),
            pltpu.SemaphoreType.DMA((3, SLOTS)),
            pltpu.SemaphoreType.DMA((3, RUNS)),
        ],
        compiler_params=pltpu.CompilerParams(collective_id=0, has_side_effects=True, vmem_limit_bytes=62 * 2**20),
    )(
        chromatograms,
        standards,
        library,
        owner_of.reshape(16, 128),
        local_group.reshape(16, 128),
        quality.reshape(16, 128),
    )


def solution(mesh):
    placed = (P("run", "prec", None), P("run", None), P(), P("prec", None), P("prec"), P("prec"))
    return jax.shard_map(
        per_device, mesh=mesh, in_specs=placed, out_specs=P("run", "prec", None), check_vma=False
    )
```

```python
import jax
import jax.numpy as jnp
from jax import lax
from jax.experimental import pallas as pl
from jax.experimental.pallas import tpu as pltpu
from jax.sharding import PartitionSpec as P

MESH = pl.DeviceIdType.MESH
F32 = jnp.float32
BF16 = jnp.bfloat16
RUNS = 8
BLOCKS = 4
BLOCK = 512
MOST = 32
OWNERS = 32
GRP = 512
HALF = GRP // 2
PTS = 256
STANDARDS = 11
SIDE = 4
SLOTS = 4
LAG = 3

LEAVES = (
    ((1, 0), ((2, 3), (3, 0), (3, 1))),
    ((0, 1), ((1, 0), (2, 0), (3, 2))),
    ((0, 3), ((0, 2), (1, 2), (2, 2))),
    ((3, 0), ((1, 3),)),
)
INNER = (((2, 1), (3, 0), 0), ((3, 3), (1, 0), 0), ((1, 1), (3, 0), 1), ((0, 3), (0, 1), 1), ((0, 1), (0, 3), 2))
ROOT = (0, 0)
NODES = tuple(n for n, _, _ in INNER) + (ROOT,)
SELF = 2 * sum(len(ps) for _, ps in LEAVES)


def layout():
    place, feeds, base = {}, {n: [n] for n in NODES}, 0
    for (sx, sz), ps in LEAVES:
        for i, (px, pz) in enumerate(ps):
            place[px, pz] = (base + i, len(ps))
            feeds[(px + sx) % SIDE, (pz + sz) % SIDE].append((px, pz))
        base += 2 * len(ps)
    for i, n in enumerate(NODES):
        place[n] = (base + i, len(NODES))
    return place, feeds


PLACE, FEEDS = layout()
CHUNKS = {n: [PLACE[p][0] + core * PLACE[p][1] for p in FEEDS[n] for core in range(2)] for n in NODES}
ORDER = [chunk for n in NODES for chunk in CHUNKS[n]]
COLUMN = {n: 128 * sum(len(CHUNKS[m]) for m in NODES[:i]) for i, n in enumerate(NODES)}


def nt_dot(a, b):
    return lax.dot_general(a, b, (((1,), (1,)), ((), ())), preferred_element_type=F32)


def to_bf16(mask):
    return mask.astype(F32).astype(BF16)


def kernel(
    x_hbm, std, lib, own, lg, q, out,
    xbuf, perm, tri, qall, qcol, srcs, tags, rtags, member, sbuf, rbuf, dbuf, ddbuf,
    x_sem, tag_ssem, tag_rsem, s_sem, r_sem, d_sem, dd_sem,
):
    yy = lax.axis_index("run")
    pp = lax.axis_index("prec")
    xx, zz, cc = pp // 8, (pp // 2) % 4, pp % 2

    def device(step, core):
        sign = 1 - 2 * core
        return (yy, ((xx + SIDE + sign * step[0]) % SIDE) * 8 + ((zz + SIDE + sign * step[1]) % SIDE) * 2 + core)

    def load(j):
        return pltpu.make_async_copy(x_hbm.at[j], xbuf.at[j % 2], x_sem.at[j % 2])

    barrier = pltpu.get_barrier_semaphore()
    for step, _ in LEAVES:
        for core in range(2):
            pl.semaphore_signal(barrier, inc=1, device_id=device(step, core), device_id_type=MESH)
    pl.semaphore_signal(barrier, inc=1, device_id=device(ROOT, 1 - cc), device_id_type=MESH)
    load(0).start()
    load(1).start()

    t = lax.broadcasted_iota(jnp.int32, (1, PTS), 1)
    later = [lib[k] <= t for k in range(1, STANDARDS - 1)]

    def pick(values):
        got = jnp.full((1, PTS), values[0], jnp.int32)
        for mask, value in zip(later, values[1:]):
            got = jnp.where(mask, value, got)
        return got.astype(F32)

    lib_at = pick([lib[k] for k in range(STANDARDS - 1)])
    lib_gap = pick([lib[k + 1] - lib[k] for k in range(STANDARDS - 1)])
    for r in range(RUNS):
        base = pick([std[r, k] for k in range(STANDARDS - 1)])
        gap = pick([std[r, k + 1] - std[r, k] for k in range(STANDARDS - 1)])
        srcs[r] = base + (t.astype(F32) - lib_at) * (gap / lib_gap)
    tri[...] = to_bf16(
        lax.broadcasted_iota(jnp.int32, (BLOCK, BLOCK), 0) < lax.broadcasted_iota(jnp.int32, (BLOCK, BLOCK), 1)
    )
    qall[...] = q[...].astype(F32)
    tags[...] = jnp.zeros_like(tags)

    def place_block(b):
        def lanes(ref):
            return jnp.concatenate([ref[pl.ds(b * 4 + i, 1), :] for i in range(4)], axis=1)

        owner = lanes(own)
        core = owner % 2
        sign = 1 - 2 * core
        px = (SIDE + sign * (xx - owner // 8)) % SIDE
        pz = (SIDE + sign * (zz - (owner // 2) % 4)) % SIDE
        chunk = jnp.zeros_like(owner)
        for (kx, kz), (start, apart) in PLACE.items():
            chunk = jnp.where((px == kx) & (pz == kz), start + core * apart, chunk)
        hit = (chunk == lax.broadcasted_iota(jnp.int32, (OWNERS, BLOCK), 0)).astype(F32)
        before = jnp.dot(hit.astype(BF16), tri[...], preferred_element_type=F32)
        rank = jnp.sum(before * hit, axis=0, keepdims=True).astype(jnp.int32)
        place = chunk * MOST + rank
        for i in range(4):
            at = lax.broadcasted_iota(jnp.int32, (256, BLOCK), 0) + i * 256
            perm[b, i * 256 : i * 256 + 256, :] = to_bf16(at == place)
        tag = lanes(lg) + 1
        low = hit * (tag % 256).astype(F32)
        high = hit * (tag // 256).astype(F32)
        at_slot = to_bf16(lax.broadcasted_iota(jnp.int32, (128, BLOCK), 0) - b * MOST == rank)
        both = nt_dot(jnp.concatenate([low, high], axis=0).astype(BF16), at_slot)
        tags[...] += jnp.broadcast_to((both[:OWNERS] + 256.0 * both[OWNERS:])[:, None, :], tags.shape)
        for i in range(4):
            weights = qall[pl.ds(b * 4 + i, 1), :]
            qcol[b, i * 128 : i * 128 + 128, :] = jnp.transpose(jnp.broadcast_to(weights, (128, 128)))

    def send_chunks(source, target, send_sem, recv_sem):
        base = 0
        for step, ps in LEAVES:
            n = len(ps)
            for core in range(2):
                pltpu.make_async_remote_copy(
                    src_ref=source.at[pl.ds(base + core * n, n)], dst_ref=target.at[pl.ds(base + cc * n, n)],
                    send_sem=send_sem, recv_sem=recv_sem, device_id=device(step, core), device_id_type=MESH,
                ).start()
            base += 2 * n
        n = len(NODES)
        mine, other = pl.ds(SELF + cc * n, n), pl.ds(SELF + (1 - cc) * n, n)
        pltpu.make_async_remote_copy(
            src_ref=source.at[other], dst_ref=target.at[mine],
            send_sem=send_sem, recv_sem=recv_sem, device_id=device(ROOT, 1 - cc), device_id_type=MESH,
        ).start()
        pltpu.make_async_copy(source.at[mine], target.at[mine], recv_sem).start()

    def wait_bytes(ref, sem):
        pltpu.make_async_copy(ref, ref, sem).wait()

    def send_profiles(j):
        slot = j % SLOTS
        load(j).wait()
        down = lax.broadcasted_iota(jnp.int32, (PTS, PTS), 0).astype(F32)
        warp = jnp.maximum(0.0, 1.0 - jnp.abs(srcs[j] - down)).astype(BF16)

        def block(b, _):
            @pl.when(j == 0)
            def _():
                place_block(b)

            rows = pl.ds(pl.multiple_of(b * BLOCK, BLOCK), BLOCK)
            seen = jnp.dot(xbuf[j % 2, rows, :], warp, preferred_element_type=F32)
            weight = qcol[b]
            logs = jnp.log(1.0 + seen)
            prof = jnp.concatenate([logs[:, :128] * weight, logs[:, 128:] * weight], axis=1).astype(BF16)
            for half in range(2):
                got = jnp.dot(perm[b, half * 512 : half * 512 + 512, :], prof, preferred_element_type=F32)
                sbuf[slot, b, half * 16 : half * 16 + 16] = got.astype(BF16).reshape(16, MOST, PTS)

            @pl.when((j == 0) & (b == 0))
            def _():
                pl.semaphore_wait(barrier, 9)

            send_chunks(sbuf.at[slot, b], rbuf.at[j, b], s_sem.at[slot], r_sem.at[j])
            return 0

        lax.fori_loop(0, BLOCKS, block, 0)

    def wait_sent(slot):
        wait_bytes(sbuf.at[slot, :, 0 : SELF + len(NODES)], s_sem.at[slot])

    def members():
        wait_bytes(rtags, tag_rsem)
        wait_bytes(tags.at[0 : SELF + len(NODES)], tag_ssem)
        group = lax.broadcasted_iota(jnp.int32, (GRP, 128), 0).astype(F32) + 1.0
        for i, chunk in enumerate(ORDER):
            member[:, i * 128 : i * 128 + 128] = to_bf16(group == rtags[chunk, 0:1, :])

    def total(j, node, half):
        rows = jnp.concatenate([rbuf[j, :, chunk].reshape(BLOCKS * MOST, PTS) for chunk in CHUNKS[node]], axis=0)
        groups = member[half * HALF : half * HALF + HALF, COLUMN[node] : COLUMN[node] + 128 * len(CHUNKS[node])]
        whole = jnp.dot(groups, rows, preferred_element_type=F32)
        for i, ((nx, nz), (sx, sz), _) in enumerate(INNER):
            if ((nx + sx) % SIDE, (nz + sz) % SIDE) == node:
                wait_bytes(ddbuf.at[j, i, half], dd_sem.at[i, half, j])
                whole = whole + ddbuf[j, i, half].astype(F32)
        return whole

    def send_sums(j, level):
        slot = j % SLOTS
        if level == 0:
            wait_bytes(rbuf.at[j], r_sem.at[j])
        for i, (node, step, at) in enumerate(INNER):
            if at == level:

                @pl.when(j >= SLOTS)
                def _(i=i):
                    wait_bytes(dbuf.at[slot, i], d_sem.at[i, slot])

                for half in range(2):
                    dbuf[slot, i, half] = total(j, node, half).astype(BF16)
                    pltpu.make_async_remote_copy(
                        src_ref=dbuf.at[slot, i, half], dst_ref=ddbuf.at[j, i, half], send_sem=d_sem.at[i, slot],
                        recv_sem=dd_sem.at[i, half, j], device_id=device(step, cc), device_id_type=MESH,
                    ).start()

    def finish(j):
        for half in range(2):
            out[j, half * HALF : half * HALF + HALF] = (0.25 * total(j, ROOT, half)).astype(BF16)

    def step(j, _):
        @pl.when(j < RUNS)
        def _():
            @pl.when(j >= SLOTS)
            def _():
                wait_sent(j % SLOTS)

            send_profiles(j)

            @pl.when(j + 2 < RUNS)
            def _():
                load(j + 2).start()

        @pl.when(j == 0)
        def _():
            send_chunks(tags, rtags, tag_ssem, tag_rsem)

        @pl.when(j == LAG - 1)
        def _():
            members()

        for level in range(3):
            @pl.when((j >= level + LAG) & (j < RUNS + level + LAG))
            def _(level=level):
                send_sums(j - level - LAG, level)

        @pl.when(j >= 3 + LAG)
        def _():
            finish(j - 3 - LAG)

        return 0

    lax.fori_loop(0, RUNS + 3 + LAG, step, 0)
    for slot in range(SLOTS):
        wait_sent(slot)
        for i in range(len(INNER)):
            wait_bytes(dbuf.at[slot, i], d_sem.at[i, slot])


def per_device(chromatograms, standards, library, owner_of, local_group, quality):
    vmem = pl.BlockSpec(memory_space=pltpu.VMEM)
    smem = pl.BlockSpec(memory_space=pltpu.SMEM)
    chunk = (OWNERS, MOST, PTS)
    return pl.pallas_call(
        kernel,
        out_shape=jax.ShapeDtypeStruct((RUNS, GRP, PTS), BF16),
        in_specs=[pl.BlockSpec(memory_space=pl.ANY), smem, smem, vmem, vmem, vmem],
        out_specs=vmem,
        scratch_shapes=[
            pltpu.VMEM((2, BLOCKS * BLOCK, PTS), BF16),
            pltpu.VMEM((BLOCKS, OWNERS * MOST, BLOCK), BF16),
            pltpu.VMEM((BLOCK, BLOCK), BF16),
            pltpu.VMEM((16, 128), F32),
            pltpu.VMEM((BLOCKS, BLOCK, 128), F32),
            pltpu.VMEM((RUNS, 1, PTS), F32),
            pltpu.VMEM((OWNERS, 8, 128), F32),
            pltpu.VMEM((OWNERS, 8, 128), F32),
            pltpu.VMEM((GRP, OWNERS * 128), BF16),
            pltpu.VMEM((SLOTS, BLOCKS, *chunk), BF16),
            pltpu.VMEM((RUNS, BLOCKS, *chunk), BF16),
            pltpu.VMEM((SLOTS, len(INNER), 2, HALF, PTS), BF16),
            pltpu.VMEM((RUNS, len(INNER), 2, HALF, PTS), BF16),
            pltpu.SemaphoreType.DMA((2,)),
            pltpu.SemaphoreType.DMA,
            pltpu.SemaphoreType.DMA,
            pltpu.SemaphoreType.DMA((SLOTS,)),
            pltpu.SemaphoreType.DMA((RUNS,)),
            pltpu.SemaphoreType.DMA((len(INNER), SLOTS)),
            pltpu.SemaphoreType.DMA((len(INNER), 2, RUNS)),
        ],
        compiler_params=pltpu.CompilerParams(collective_id=0, has_side_effects=True, vmem_limit_bytes=62 * 2**20),
    )(
        chromatograms,
        standards,
        library,
        owner_of.reshape(16, 128),
        local_group.reshape(16, 128),
        quality.reshape(16, 128),
    )


def solution(mesh):
    placed = (P("run", "prec", None), P("run", None), P(), P("prec", None), P("prec"), P("prec"))
    return jax.shard_map(
        per_device, mesh=mesh, in_specs=placed, out_specs=P("run", "prec", None), check_vma=False
    )
```

```python
import jax
import jax.numpy as jnp
from jax import lax
from jax.experimental import pallas as pl
from jax.experimental.pallas import tpu as pltpu
from jax.sharding import PartitionSpec as P

MESH = pl.DeviceIdType.MESH
F32 = jnp.float32
BF16 = jnp.bfloat16
RUNS = 8
BLOCKS = 4
BLOCK = 512
MOST = 32
OWNERS = 32
GRP = 512
HALF = GRP // 2
PTS = 256
STANDARDS = 11
SIDE = 4
LINE = 8
OTHERS = 13


def nt_dot(a, b):
    return lax.dot_general(a, b, (((1,), (1,)), ((), ())), preferred_element_type=F32)


def to_bf16(mask):
    return mask.astype(F32).astype(BF16)


def wait_bytes(ref, sem):
    pltpu.make_async_copy(ref, ref, sem).wait()


def kernel(
    x_hbm, std, lib, own, lg, q, out,
    xbuf, tri, qcol, srcs, info, infos, pbuf, rows, slots, tagbuf, member, dbuf, relay, sums, mine, fbuf,
    x_sem, info_ssem, info_rsem, s_sem, r_sem, d_sem, relay_sem, sums_sem, f_sem, out_sem,
):
    yy = lax.axis_index("run")
    pp = lax.axis_index("prec")
    xx, zz, cc = pp // 8, (pp // 2) % 4, pp % 2
    first = (1 - cc) * xx + cc * zz
    second = (1 - cc) * zz + cc * xx
    my_run = cc * SIDE + first

    def prec(order, a, b, core):
        return ((1 - order) * a + order * b) * 8 + ((1 - order) * b + order * a) * 2 + core

    def remote(src, dst, send_sem, recv_sem, target):
        pltpu.make_async_remote_copy(
            src_ref=src, dst_ref=dst, send_sem=send_sem, recv_sem=recv_sem, device_id=(yy, target), device_id_type=MESH
        ).start()

    def turn(k):
        return jnp.where(k == 0, 2, jnp.where(k == 1, 0, jnp.where(k == 2, 1, 3)))

    def job(i):
        order, df = i % 2, turn(i // 2)
        a = (1 - order) * xx + order * zz
        b = (1 - order) * zz + order * xx
        to = (a + df) % SIDE
        return order, order * SIDE + to, prec(order, to, b, order), a * 2 + cc

    def load(i):
        return pltpu.make_async_copy(x_hbm.at[job(i)[1]], xbuf.at[i % 2], x_sem.at[i % 2])

    def is_mine(i):
        return i == 2 + cc

    barrier = pltpu.get_barrier_semaphore()
    for step in range(SIDE):
        for core in range(2):
            if step:
                for other in (prec(0, (xx + step) % SIDE, zz, core), prec(0, xx, (zz + step) % SIDE, core)):
                    pl.semaphore_signal(barrier, inc=1, device_id=(yy, other), device_id_type=MESH)
    pl.semaphore_signal(barrier, inc=1, device_id=(yy, prec(0, xx, zz, 1 - cc)), device_id_type=MESH)
    load(0).start()
    load(1).start()
    info[0] = own[...]
    info[1] = lg[...]

    t = lax.broadcasted_iota(jnp.int32, (1, PTS), 1)
    later = [lib[k] <= t for k in range(1, STANDARDS - 1)]

    def pick(values):
        got = jnp.full((1, PTS), values[0], jnp.int32)
        for mask, value in zip(later, values[1:]):
            got = jnp.where(mask, value, got)
        return got.astype(F32)

    lib_at = pick([lib[k] for k in range(STANDARDS - 1)])
    lib_gap = pick([lib[k + 1] - lib[k] for k in range(STANDARDS - 1)])
    for r in range(RUNS):
        base = pick([std[r, k] for k in range(STANDARDS - 1)])
        gap = pick([std[r, k + 1] - std[r, k] for k in range(STANDARDS - 1)])
        srcs[r] = base + (t.astype(F32) - lib_at) * (gap / lib_gap)
    tri[...] = to_bf16(
        lax.broadcasted_iota(jnp.int32, (BLOCK, BLOCK), 0) < lax.broadcasted_iota(jnp.int32, (BLOCK, BLOCK), 1)
    )
    weights = q[...].astype(F32)
    for i in range(16):
        qcol[i * 128 : i * 128 + 128, :] = jnp.transpose(jnp.broadcast_to(weights[i : i + 1, :], (128, 128)))

    def start(i, b):
        _, _, target, place = job(i)
        remote(pbuf.at[i, b], rows.at[place, b], s_sem.at[i, b], r_sem.at[place, b], target)

    def sent(i, b):
        wait_bytes(pbuf.at[i, b], s_sem.at[i, b])

    def send_run(i, _):
        _, run, target, place = job(i)
        load(i).wait()
        down = lax.broadcasted_iota(jnp.int32, (PTS, PTS), 0).astype(F32)
        warp = jnp.maximum(0.0, 1.0 - jnp.abs(srcs[run] - down)).astype(BF16)

        def block(b, _):
            at = pl.ds(pl.multiple_of(b * BLOCK, BLOCK), BLOCK)
            seen = jnp.dot(xbuf[i % 2, at, :], warp, preferred_element_type=F32)
            weight = qcol[at, :]
            logs = jnp.log(1.0 + seen)
            pbuf[i, b] = jnp.concatenate([logs[:, :128] * weight, logs[:, 128:] * weight], axis=1).astype(BF16)

            @pl.when((i == 0) & (b == 0))
            def _():
                pl.semaphore_wait(barrier, OTHERS)

            @pl.when(is_mine(i))
            def _():
                pltpu.make_async_copy(pbuf.at[i, b], rows.at[place, b], r_sem.at[place, b]).start()

            @pl.when((i < SIDE) & jnp.logical_not(is_mine(i)))
            def _():
                start(i, b)

            return 0

        lax.fori_loop(0, BLOCKS, block, 0)

        @pl.when(is_mine(i))
        def _():
            pltpu.make_async_copy(info, infos.at[place], info_rsem).start()

        @pl.when(jnp.logical_not(is_mine(i)))
        def _():
            remote(info, infos.at[place], info_ssem, info_rsem, target)

        @pl.when(i + 2 < RUNS)
        def _():
            load(i + 2).start()

        return 0

    lax.fori_loop(0, RUNS, send_run, 0)

    wait_bytes(infos, info_rsem)

    def to_slots(df, core, b):
        src = ((first + SIDE - df) % SIDE) * 2 + core

        def lanes(which):
            return jnp.concatenate([infos[src, which, pl.ds(b * 4 + i, 1), :] for i in range(4)], axis=1)

        owner = lanes(0)
        hit = (owner == lax.broadcasted_iota(jnp.int32, (OWNERS, BLOCK), 0)).astype(F32)
        before = jnp.dot(hit.astype(BF16), tri[...], preferred_element_type=F32)
        rank = jnp.sum(before * hit, axis=0, keepdims=True).astype(jnp.int32)
        tag = lanes(1) + 1
        low = hit * (tag % 256).astype(F32)
        high = hit * (tag // 256).astype(F32)
        at_slot = to_bf16(lax.broadcasted_iota(jnp.int32, (128, BLOCK), 0) - b * MOST == rank)
        both = nt_dot(jnp.concatenate([low, high], axis=0).astype(BF16), at_slot)
        tags = both[:OWNERS] + 256.0 * both[OWNERS:]

        @pl.when(b == 0)
        def _():
            tagbuf[src] = tags

        @pl.when(b > 0)
        def _():
            tagbuf[src] += tags

        place = owner * MOST + rank
        wait_bytes(rows.at[src, b], r_sem.at[src, b])
        for i in range(4):
            at = lax.broadcasted_iota(jnp.int32, (256, BLOCK), 0) + i * 256
            got = jnp.dot(to_bf16(at == place), rows[src, b], preferred_element_type=F32)
            slots[i * 8 : i * 8 + 8, src, b] = got.astype(BF16).reshape(8, MOST, PTS)

    def whole_chip(df):
        def one(n, _):
            to_slots(df, n // BLOCKS, n % BLOCKS)
            return 0

        lax.fori_loop(0, 2 * BLOCKS, one, 0)

    def send_near(b):
        for i in range(SIDE, RUNS):
            start(i, b)

    whole_chip(0)
    for i in range(2):
        for b in range(BLOCKS):
            sent(i, b)
    send_near(0)
    send_near(1)
    whole_chip(2)

    def near_block(b, _):
        @pl.when(b < 2)
        def _():
            for i in range(SIDE, RUNS):
                sent(i, b)
            send_near(b + 2)

        def one(n, _):
            to_slots(1 + 2 * (n // 2), n % 2, b)
            return 0

        lax.fori_loop(0, SIDE, one, 0)
        return 0

    lax.fori_loop(0, BLOCKS, near_block, 0)

    def total(s, t):
        o = prec(cc, t // 2, s, t % 2)
        group = lax.broadcasted_iota(jnp.int32, (GRP, 128), 0).astype(F32) + 1.0
        for src in range(LINE):
            member[:, src * 128 : src * 128 + 128] = to_bf16(group == tagbuf[src, pl.ds(o, 1), :])
        return jnp.dot(member[...], slots[o].reshape(LINE * BLOCKS * MOST, PTS), preferred_element_type=F32)

    def beside(step):
        return prec(cc, first, (second + step) % SIDE, cc)

    def far(t, _):
        whole = total((second + 2) % SIDE, t).astype(BF16)
        for half in range(2):
            dbuf[0, t, half] = whole[half * HALF : half * HALF + HALF]
            remote(dbuf.at[0, t, half], relay.at[half, t], d_sem, relay_sem.at[half, t], beside((1, 3)[half]))
        return 0

    lax.fori_loop(0, LINE, far, 0)

    def near(t, _):
        for half in range(2):
            step = (1, 3)[half]
            whole = total((second + step) % SIDE, t)
            wait_bytes(relay.at[half, t], relay_sem.at[half, t])
            passed = whole[half * HALF : half * HALF + HALF] + relay[half, t].astype(F32)
            dbuf[1 + half, t, half] = passed.astype(BF16)
            dbuf[1 + half, t, 1 - half] = whole[(1 - half) * HALF : (1 - half) * HALF + HALF].astype(BF16)
            remote(dbuf.at[1 + half, t], sums.at[half, t], d_sem, sums_sem.at[half, t], beside(step))
        return 0

    lax.fori_loop(0, LINE, near, 0)

    def keep(t, _):
        mine[t] = total(second, t)
        return 0

    lax.fori_loop(0, LINE, keep, 0)

    def finish(t, _):
        whole = mine[t].reshape(2, HALF, PTS)
        for half in range(2):
            wait_bytes(sums.at[half, t], sums_sem.at[half, t])
            whole = whole + sums[half, t].astype(F32)
        done = (0.25 * whole).astype(BF16).reshape(GRP, PTS)
        here = t == first * 2 + cc

        @pl.when(here)
        def _():
            out[my_run] = done

        @pl.when(jnp.logical_not(here))
        def _():
            fbuf[t] = done
            remote(fbuf.at[t], out.at[my_run], f_sem, out_sem, prec(cc, t // 2, second, t % 2))

        return 0

    lax.fori_loop(0, LINE, finish, 0)

    wait_bytes(out.at[0 : RUNS - 1], out_sem)
    wait_bytes(fbuf.at[0 : LINE - 1], f_sem)
    wait_bytes(dbuf, d_sem)
    wait_bytes(infos.at[0 : LINE - 1], info_ssem)

    for b in range(BLOCKS):
        sent(3 - cc, b)
    for i in range(SIDE, RUNS):
        for b in (2, 3):
            sent(i, b)


def per_device(chromatograms, standards, library, owner_of, local_group, quality):
    vmem = pl.BlockSpec(memory_space=pltpu.VMEM)
    smem = pl.BlockSpec(memory_space=pltpu.SMEM)
    return pl.pallas_call(
        kernel,
        out_shape=pltpu.VMEM((RUNS, GRP, PTS), BF16),
        in_specs=[pl.BlockSpec(memory_space=pl.ANY), smem, smem, vmem, vmem, vmem],
        out_specs=vmem,
        scratch_shapes=[
            pltpu.VMEM((2, BLOCKS * BLOCK, PTS), BF16),
            pltpu.VMEM((BLOCK, BLOCK), BF16),
            pltpu.VMEM((BLOCKS * BLOCK, 128), F32),
            pltpu.VMEM((RUNS, 1, PTS), F32),
            pltpu.VMEM((2, 16, 128), jnp.int32),
            pltpu.VMEM((LINE, 2, 16, 128), jnp.int32),
            pltpu.VMEM((RUNS, BLOCKS, BLOCK, PTS), BF16),
            pltpu.VMEM((LINE, BLOCKS, BLOCK, PTS), BF16),
            pltpu.VMEM((OWNERS, LINE, BLOCKS, MOST, PTS), BF16),
            pltpu.VMEM((LINE, OWNERS, 128), F32),
            pltpu.VMEM((GRP, LINE * 128), BF16),
            pltpu.VMEM((3, LINE, 2, HALF, PTS), BF16),
            pltpu.VMEM((2, LINE, HALF, PTS), BF16),
            pltpu.VMEM((2, LINE, 2, HALF, PTS), BF16),
            pltpu.VMEM((LINE, GRP, PTS), F32),
            pltpu.VMEM((LINE, GRP, PTS), BF16),
            pltpu.SemaphoreType.DMA((2,)),
            pltpu.SemaphoreType.DMA,
            pltpu.SemaphoreType.DMA,
            pltpu.SemaphoreType.DMA((RUNS, BLOCKS)),
            pltpu.SemaphoreType.DMA((LINE, BLOCKS)),
            pltpu.SemaphoreType.DMA,
            pltpu.SemaphoreType.DMA((2, LINE)),
            pltpu.SemaphoreType.DMA((2, LINE)),
            pltpu.SemaphoreType.DMA,
            pltpu.SemaphoreType.DMA,
        ],
        compiler_params=pltpu.CompilerParams(collective_id=0, has_side_effects=True, vmem_limit_bytes=58 * 2**20),
    )(
        chromatograms,
        standards,
        library,
        owner_of.reshape(16, 128),
        local_group.reshape(16, 128),
        quality.reshape(16, 128),
    )


def solution(mesh):
    placed = (P("run", "prec", None), P("run", None), P(), P("prec", None), P("prec"), P("prec"))
    return jax.shard_map(
        per_device, mesh=mesh, in_specs=placed, out_specs=P("run", "prec", None), check_vma=False
    )
```

```python
import jax
import jax.numpy as jnp
from jax import lax
from jax.experimental import pallas as pl
from jax.experimental.pallas import tpu as pltpu
from jax.sharding import PartitionSpec as P

MESH = pl.DeviceIdType.MESH
F32 = jnp.float32
BF16 = jnp.bfloat16
RUNS = 8
BLOCKS = 4
BLOCK = 512
MOST = 32
OWNERS = 32
GRP = 512
HALF = GRP // 2
PTS = 256
STANDARDS = 11
SIDE = 4
LINE = 8
OTHERS = 13


def nt_dot(a, b):
    return lax.dot_general(a, b, (((1,), (1,)), ((), ())), preferred_element_type=F32)


def to_bf16(mask):
    return mask.astype(F32).astype(BF16)


def wait_bytes(ref, sem):
    pltpu.make_async_copy(ref, ref, sem).wait()


def kernel(
    x_hbm, std, lib, own, lg, q, out,
    xbuf, tri, qcol, srcs, info, infos, pbuf, rows, slots, tagbuf, member, dbuf, relay, sums, mine, fbuf,
    x_sem, info_ssem, info_rsem, s_sem, r_sem, d_sem, relay_sem, sums_sem, f_sem, out_sem,
):
    yy = lax.axis_index("run")
    pp = lax.axis_index("prec")
    xx, zz, cc = pp // 8, (pp // 2) % 4, pp % 2
    first = (1 - cc) * xx + cc * zz
    second = (1 - cc) * zz + cc * xx
    my_run = cc * SIDE + first

    def prec(order, a, b, core):
        return ((1 - order) * a + order * b) * 8 + ((1 - order) * b + order * a) * 2 + core

    def remote(src, dst, send_sem, recv_sem, target):
        pltpu.make_async_remote_copy(
            src_ref=src, dst_ref=dst, send_sem=send_sem, recv_sem=recv_sem, device_id=(yy, target), device_id_type=MESH
        ).start()

    def turn(k):
        return jnp.where(k == 0, 2, jnp.where(k == 1, 0, jnp.where(k == 2, 1, 3)))

    def job(i):
        order, df = i % 2, turn(i // 2)
        a = (1 - order) * xx + order * zz
        b = (1 - order) * zz + order * xx
        to = (a + df) % SIDE
        return order, order * SIDE + to, prec(order, to, b, order), a * 2 + cc

    def load(i):
        return pltpu.make_async_copy(x_hbm.at[job(i)[1]], xbuf.at[i % 2], x_sem.at[i % 2])

    def is_mine(i):
        return i == 2 + cc

    barrier = pltpu.get_barrier_semaphore()
    for step in range(SIDE):
        for core in range(2):
            if step:
                for other in (prec(0, (xx + step) % SIDE, zz, core), prec(0, xx, (zz + step) % SIDE, core)):
                    pl.semaphore_signal(barrier, inc=1, device_id=(yy, other), device_id_type=MESH)
    pl.semaphore_signal(barrier, inc=1, device_id=(yy, prec(0, xx, zz, 1 - cc)), device_id_type=MESH)
    load(0).start()
    load(1).start()
    info[0] = own[...]
    info[1] = lg[...]

    t = lax.broadcasted_iota(jnp.int32, (1, PTS), 1)
    later = [lib[k] <= t for k in range(1, STANDARDS - 1)]

    def pick(values):
        got = jnp.full((1, PTS), values[0], jnp.int32)
        for mask, value in zip(later, values[1:]):
            got = jnp.where(mask, value, got)
        return got.astype(F32)

    lib_at = pick([lib[k] for k in range(STANDARDS - 1)])
    lib_gap = pick([lib[k + 1] - lib[k] for k in range(STANDARDS - 1)])
    for r in range(RUNS):
        base = pick([std[r, k] for k in range(STANDARDS - 1)])
        gap = pick([std[r, k + 1] - std[r, k] for k in range(STANDARDS - 1)])
        srcs[r] = base + (t.astype(F32) - lib_at) * (gap / lib_gap)
    tri[...] = to_bf16(
        lax.broadcasted_iota(jnp.int32, (BLOCK, BLOCK), 0) < lax.broadcasted_iota(jnp.int32, (BLOCK, BLOCK), 1)
    )
    weights = q[...].astype(F32)
    for i in range(16):
        qcol[i * 128 : i * 128 + 128, :] = jnp.transpose(jnp.broadcast_to(weights[i : i + 1, :], (128, 128)))

    def start(i, b):
        _, _, target, place = job(i)
        remote(pbuf.at[i, b], rows.at[place, b], s_sem.at[i, b], r_sem.at[place, b], target)

    def sent(i, b):
        wait_bytes(pbuf.at[i, b], s_sem.at[i, b])

    def send_run(i, _):
        _, run, target, place = job(i)
        load(i).wait()
        down = lax.broadcasted_iota(jnp.int32, (PTS, PTS), 0).astype(F32)
        warp = jnp.maximum(0.0, 1.0 - jnp.abs(srcs[run] - down)).astype(BF16)

        def block(b, _):
            at = pl.ds(pl.multiple_of(b * BLOCK, BLOCK), BLOCK)
            seen = jnp.dot(xbuf[i % 2, at, :], warp, preferred_element_type=F32)
            weight = qcol[at, :]
            logs = jnp.log(1.0 + seen)
            pbuf[i, b] = jnp.concatenate([logs[:, :128] * weight, logs[:, 128:] * weight], axis=1).astype(BF16)

            @pl.when((i == 0) & (b == 0))
            def _():
                pl.semaphore_wait(barrier, OTHERS)

            @pl.when(is_mine(i))
            def _():
                pltpu.make_async_copy(pbuf.at[i, b], rows.at[place, b], r_sem.at[place, b]).start()

            @pl.when((i < SIDE) & jnp.logical_not(is_mine(i)))
            def _():
                start(i, b)

            return 0

        lax.fori_loop(0, BLOCKS, block, 0)

        @pl.when(is_mine(i))
        def _():
            pltpu.make_async_copy(info, infos.at[place], info_rsem).start()

        @pl.when(jnp.logical_not(is_mine(i)))
        def _():
            remote(info, infos.at[place], info_ssem, info_rsem, target)

        @pl.when(i + 2 < RUNS)
        def _():
            load(i + 2).start()

        return 0

    lax.fori_loop(0, RUNS, send_run, 0)

    wait_bytes(infos, info_rsem)

    def to_slots(df, core, b):
        src = ((first + SIDE - df) % SIDE) * 2 + core

        def lanes(which):
            return jnp.concatenate([infos[src, which, pl.ds(b * 4 + i, 1), :] for i in range(4)], axis=1)

        owner = lanes(0)
        hit = (owner == lax.broadcasted_iota(jnp.int32, (OWNERS, BLOCK), 0)).astype(F32)
        before = jnp.dot(hit.astype(BF16), tri[...], preferred_element_type=F32)
        rank = jnp.sum(before * hit, axis=0, keepdims=True).astype(jnp.int32)
        tag = lanes(1) + 1
        low = hit * (tag % 256).astype(F32)
        high = hit * (tag // 256).astype(F32)
        at_slot = to_bf16(lax.broadcasted_iota(jnp.int32, (128, BLOCK), 0) - b * MOST == rank)
        both = nt_dot(jnp.concatenate([low, high], axis=0).astype(BF16), at_slot)
        tags = both[:OWNERS] + 256.0 * both[OWNERS:]

        @pl.when(b == 0)
        def _():
            tagbuf[src] = tags

        @pl.when(b > 0)
        def _():
            tagbuf[src] += tags

        place = owner * MOST + rank
        wait_bytes(rows.at[src, b], r_sem.at[src, b])
        for i in range(4):
            at = lax.broadcasted_iota(jnp.int32, (256, BLOCK), 0) + i * 256
            got = jnp.dot(to_bf16(at == place), rows[src, b], preferred_element_type=F32)
            slots[i * 8 : i * 8 + 8, src, b] = got.astype(BF16).reshape(8, MOST, PTS)

    def whole_chip(df):
        def one(n, _):
            to_slots(df, n // BLOCKS, n % BLOCKS)
            return 0

        lax.fori_loop(0, 2 * BLOCKS, one, 0)

    def send_near(b):
        for i in range(SIDE, RUNS):
            start(i, b)

    whole_chip(0)
    for i in range(2):
        for b in range(BLOCKS):
            sent(i, b)
    send_near(0)
    send_near(1)
    whole_chip(2)

    def near_block(b, _):
        @pl.when(b < 2)
        def _():
            for i in range(SIDE, RUNS):
                sent(i, b)
            send_near(b + 2)

        def one(n, _):
            to_slots(1 + 2 * (n // 2), n % 2, b)
            return 0

        lax.fori_loop(0, SIDE, one, 0)
        return 0

    lax.fori_loop(0, BLOCKS, near_block, 0)

    def total(s, t):
        o = prec(cc, t // 2, s, t % 2)
        group = lax.broadcasted_iota(jnp.int32, (GRP, 128), 0).astype(F32) + 1.0
        for src in range(LINE):
            member[:, src * 128 : src * 128 + 128] = to_bf16(group == tagbuf[src, pl.ds(o, 1), :])
        return jnp.dot(member[...], slots[o].reshape(LINE * BLOCKS * MOST, PTS), preferred_element_type=F32)

    def beside(step):
        return prec(cc, first, (second + step) % SIDE, cc)

    def served(n):
        return ((first + turn(n // 2)) % SIDE) * 2 + n % 2

    def far(n, _):
        t = served(n)
        whole = total((second + 2) % SIDE, t).astype(BF16)
        for half in range(2):
            dbuf[0, t, half] = whole[half * HALF : half * HALF + HALF]
            remote(dbuf.at[0, t, half], relay.at[half, t], d_sem, relay_sem.at[half, t], beside((1, 3)[half]))
        return 0

    lax.fori_loop(0, LINE, far, 0)

    def near(n, _):
        t = served(n)
        for half in range(2):
            step = (1, 3)[half]
            whole = total((second + step) % SIDE, t)
            wait_bytes(relay.at[half, t], relay_sem.at[half, t])
            passed = whole[half * HALF : half * HALF + HALF] + relay[half, t].astype(F32)
            dbuf[1 + half, t, half] = passed.astype(BF16)
            dbuf[1 + half, t, 1 - half] = whole[(1 - half) * HALF : (1 - half) * HALF + HALF].astype(BF16)
            remote(dbuf.at[1 + half, t], sums.at[half, t], d_sem, sums_sem.at[half, t], beside(step))
        return 0

    lax.fori_loop(0, LINE, near, 0)

    def keep(t, _):
        mine[t] = total(second, t)
        return 0

    lax.fori_loop(0, LINE, keep, 0)

    def finish(n, _):
        t = served(n)
        whole = mine[t].reshape(2, HALF, PTS)
        for half in range(2):
            wait_bytes(sums.at[half, t], sums_sem.at[half, t])
            whole = whole + sums[half, t].astype(F32)
        done = (0.25 * whole).astype(BF16).reshape(GRP, PTS)
        here = t == first * 2 + cc

        @pl.when(here)
        def _():
            out[my_run] = done

        @pl.when(jnp.logical_not(here))
        def _():
            fbuf[t] = done
            remote(fbuf.at[t], out.at[my_run], f_sem, out_sem, prec(cc, t // 2, second, t % 2))

        return 0

    lax.fori_loop(0, LINE, finish, 0)

    wait_bytes(out.at[0 : RUNS - 1], out_sem)
    wait_bytes(fbuf.at[0 : LINE - 1], f_sem)
    wait_bytes(dbuf, d_sem)
    wait_bytes(infos.at[0 : LINE - 1], info_ssem)

    for b in range(BLOCKS):
        sent(3 - cc, b)
    for i in range(SIDE, RUNS):
        for b in (2, 3):
            sent(i, b)


def per_device(chromatograms, standards, library, owner_of, local_group, quality):
    vmem = pl.BlockSpec(memory_space=pltpu.VMEM)
    smem = pl.BlockSpec(memory_space=pltpu.SMEM)
    return pl.pallas_call(
        kernel,
        out_shape=pltpu.VMEM((RUNS, GRP, PTS), BF16),
        in_specs=[pl.BlockSpec(memory_space=pl.ANY), smem, smem, vmem, vmem, vmem],
        out_specs=vmem,
        scratch_shapes=[
            pltpu.VMEM((2, BLOCKS * BLOCK, PTS), BF16),
            pltpu.VMEM((BLOCK, BLOCK), BF16),
            pltpu.VMEM((BLOCKS * BLOCK, 128), F32),
            pltpu.VMEM((RUNS, 1, PTS), F32),
            pltpu.VMEM((2, 16, 128), jnp.int32),
            pltpu.VMEM((LINE, 2, 16, 128), jnp.int32),
            pltpu.VMEM((RUNS, BLOCKS, BLOCK, PTS), BF16),
            pltpu.VMEM((LINE, BLOCKS, BLOCK, PTS), BF16),
            pltpu.VMEM((OWNERS, LINE, BLOCKS, MOST, PTS), BF16),
            pltpu.VMEM((LINE, OWNERS, 128), F32),
            pltpu.VMEM((GRP, LINE * 128), BF16),
            pltpu.VMEM((3, LINE, 2, HALF, PTS), BF16),
            pltpu.VMEM((2, LINE, HALF, PTS), BF16),
            pltpu.VMEM((2, LINE, 2, HALF, PTS), BF16),
            pltpu.VMEM((LINE, GRP, PTS), F32),
            pltpu.VMEM((LINE, GRP, PTS), BF16),
            pltpu.SemaphoreType.DMA((2,)),
            pltpu.SemaphoreType.DMA,
            pltpu.SemaphoreType.DMA,
            pltpu.SemaphoreType.DMA((RUNS, BLOCKS)),
            pltpu.SemaphoreType.DMA((LINE, BLOCKS)),
            pltpu.SemaphoreType.DMA,
            pltpu.SemaphoreType.DMA((2, LINE)),
            pltpu.SemaphoreType.DMA((2, LINE)),
            pltpu.SemaphoreType.DMA,
            pltpu.SemaphoreType.DMA,
        ],
        compiler_params=pltpu.CompilerParams(collective_id=0, has_side_effects=True, vmem_limit_bytes=58 * 2**20),
    )(
        chromatograms,
        standards,
        library,
        owner_of.reshape(16, 128),
        local_group.reshape(16, 128),
        quality.reshape(16, 128),
    )


def solution(mesh):
    placed = (P("run", "prec", None), P("run", None), P(), P("prec", None), P("prec"), P("prec"))
    return jax.shard_map(
        per_device, mesh=mesh, in_specs=placed, out_specs=P("run", "prec", None), check_vma=False
    )
```

```python
import jax
import jax.numpy as jnp
from jax import lax
from jax.experimental import pallas as pl
from jax.experimental.pallas import tpu as pltpu
from jax.sharding import PartitionSpec as P

MESH = pl.DeviceIdType.MESH
F32 = jnp.float32
BF16 = jnp.bfloat16
RUNS = 8
BLOCKS = 4
BLOCK = 512
MOST = 32
OWNERS = 32
GRP = 512
HALF = GRP // 2
PTS = 256
STANDARDS = 11
SIDE = 4
LINE = 8
OTHERS = 13
BEHIND = 3


def nt_dot(a, b):
    return lax.dot_general(a, b, (((1,), (1,)), ((), ())), preferred_element_type=F32)


def to_bf16(mask):
    return mask.astype(F32).astype(BF16)


def wait_bytes(ref, sem):
    pltpu.make_async_copy(ref, ref, sem).wait()


def kernel(
    x_hbm, std, lib, own, lg, q, out,
    xbuf, tri, qcol, srcs, info, infos, pbuf, rows, slots, tagbuf, member, dbuf, relay, sums, mine, fbuf,
    x_sem, info_ssem, info_rsem, s_sem, r_sem, d_sem, near_sem, relay_sem, sums_sem, f_sem, out_sem,
):
    yy = lax.axis_index("run")
    pp = lax.axis_index("prec")
    xx, zz, cc = pp // 8, (pp // 2) % 4, pp % 2
    first = (1 - cc) * xx + cc * zz
    second = (1 - cc) * zz + cc * xx
    my_run = cc * SIDE + first

    def prec(order, a, b, core):
        return ((1 - order) * a + order * b) * 8 + ((1 - order) * b + order * a) * 2 + core

    def remote(src, dst, send_sem, recv_sem, target):
        pltpu.make_async_remote_copy(
            src_ref=src, dst_ref=dst, send_sem=send_sem, recv_sem=recv_sem, device_id=(yy, target), device_id_type=MESH
        ).start()

    def turn(k):
        return jnp.where(k == 0, 2, jnp.where(k == 1, 0, jnp.where(k == 2, 1, 3)))

    def job(i):
        order, df = i % 2, turn(i // 2)
        a = (1 - order) * xx + order * zz
        b = (1 - order) * zz + order * xx
        to = (a + df) % SIDE
        return order, order * SIDE + to, prec(order, to, b, order), a * 2 + cc

    def load(i):
        return pltpu.make_async_copy(x_hbm.at[job(i)[1]], xbuf.at[i % 2], x_sem.at[i % 2])

    def is_mine(i):
        return i == 2 + cc

    barrier = pltpu.get_barrier_semaphore()
    for step in range(SIDE):
        for core in range(2):
            if step:
                for other in (prec(0, (xx + step) % SIDE, zz, core), prec(0, xx, (zz + step) % SIDE, core)):
                    pl.semaphore_signal(barrier, inc=1, device_id=(yy, other), device_id_type=MESH)
    pl.semaphore_signal(barrier, inc=1, device_id=(yy, prec(0, xx, zz, 1 - cc)), device_id_type=MESH)
    load(0).start()
    load(1).start()
    info[0] = own[...]
    info[1] = lg[...]

    t = lax.broadcasted_iota(jnp.int32, (1, PTS), 1)
    later = [lib[k] <= t for k in range(1, STANDARDS - 1)]

    def pick(values):
        got = jnp.full((1, PTS), values[0], jnp.int32)
        for mask, value in zip(later, values[1:]):
            got = jnp.where(mask, value, got)
        return got.astype(F32)

    lib_at = pick([lib[k] for k in range(STANDARDS - 1)])
    lib_gap = pick([lib[k + 1] - lib[k] for k in range(STANDARDS - 1)])
    for r in range(RUNS):
        base = pick([std[r, k] for k in range(STANDARDS - 1)])
        gap = pick([std[r, k + 1] - std[r, k] for k in range(STANDARDS - 1)])
        srcs[r] = base + (t.astype(F32) - lib_at) * (gap / lib_gap)
    tri[...] = to_bf16(
        lax.broadcasted_iota(jnp.int32, (BLOCK, BLOCK), 0) < lax.broadcasted_iota(jnp.int32, (BLOCK, BLOCK), 1)
    )
    weights = q[...].astype(F32)
    for i in range(16):
        qcol[i * 128 : i * 128 + 128, :] = jnp.transpose(jnp.broadcast_to(weights[i : i + 1, :], (128, 128)))

    def start(i, b):
        _, _, target, place = job(i)
        remote(pbuf.at[i, b], rows.at[place, b], s_sem.at[i, b], r_sem.at[place, b], target)

    def sent(i, b):
        wait_bytes(pbuf.at[i, b], s_sem.at[i, b])

    def send_run(i, _):
        _, run, target, place = job(i)
        load(i).wait()
        down = lax.broadcasted_iota(jnp.int32, (PTS, PTS), 0).astype(F32)
        warp = jnp.maximum(0.0, 1.0 - jnp.abs(srcs[run] - down)).astype(BF16)

        def block(b, _):
            at = pl.ds(pl.multiple_of(b * BLOCK, BLOCK), BLOCK)
            seen = jnp.dot(xbuf[i % 2, at, :], warp, preferred_element_type=F32)
            weight = qcol[at, :]
            logs = jnp.log(1.0 + seen)
            pbuf[i, b] = jnp.concatenate([logs[:, :128] * weight, logs[:, 128:] * weight], axis=1).astype(BF16)

            @pl.when((i == 0) & (b == 0))
            def _():
                pl.semaphore_wait(barrier, OTHERS)

            @pl.when(is_mine(i))
            def _():
                pltpu.make_async_copy(pbuf.at[i, b], rows.at[place, b], r_sem.at[place, b]).start()

            @pl.when((i < SIDE) & jnp.logical_not(is_mine(i)))
            def _():
                start(i, b)

            return 0

        lax.fori_loop(0, BLOCKS, block, 0)

        @pl.when(is_mine(i))
        def _():
            pltpu.make_async_copy(info, infos.at[place], info_rsem).start()

        @pl.when(jnp.logical_not(is_mine(i)))
        def _():
            remote(info, infos.at[place], info_ssem, info_rsem, target)

        @pl.when(i + 2 < RUNS)
        def _():
            load(i + 2).start()

        return 0

    lax.fori_loop(0, RUNS, send_run, 0)

    wait_bytes(infos, info_rsem)

    def to_slots(df, core, b):
        src = ((first + SIDE - df) % SIDE) * 2 + core

        def lanes(which):
            return jnp.concatenate([infos[src, which, pl.ds(b * 4 + i, 1), :] for i in range(4)], axis=1)

        owner = lanes(0)
        hit = (owner == lax.broadcasted_iota(jnp.int32, (OWNERS, BLOCK), 0)).astype(F32)
        before = jnp.dot(hit.astype(BF16), tri[...], preferred_element_type=F32)
        rank = jnp.sum(before * hit, axis=0, keepdims=True).astype(jnp.int32)
        tag = lanes(1) + 1
        low = hit * (tag % 256).astype(F32)
        high = hit * (tag // 256).astype(F32)
        at_slot = to_bf16(lax.broadcasted_iota(jnp.int32, (128, BLOCK), 0) - b * MOST == rank)
        both = nt_dot(jnp.concatenate([low, high], axis=0).astype(BF16), at_slot)
        tags = both[:OWNERS] + 256.0 * both[OWNERS:]

        @pl.when(b == 0)
        def _():
            tagbuf[src] = tags

        @pl.when(b > 0)
        def _():
            tagbuf[src] += tags

        place = owner * MOST + rank
        wait_bytes(rows.at[src, b], r_sem.at[src, b])
        for i in range(4):
            at = lax.broadcasted_iota(jnp.int32, (256, BLOCK), 0) + i * 256
            got = jnp.dot(to_bf16(at == place), rows[src, b], preferred_element_type=F32)
            slots[i * 8 : i * 8 + 8, src, b] = got.astype(BF16).reshape(8, MOST, PTS)

    def whole_chip(df):
        def one(n, _):
            to_slots(df, n // BLOCKS, n % BLOCKS)
            return 0

        lax.fori_loop(0, 2 * BLOCKS, one, 0)

    def send_near(b):
        for i in range(SIDE, RUNS):
            start(i, b)

    whole_chip(0)
    for i in range(2):
        for b in range(BLOCKS):
            sent(i, b)
    send_near(0)
    send_near(1)
    whole_chip(2)

    def near_block(b, _):
        @pl.when(b < 2)
        def _():
            for i in range(SIDE, RUNS):
                sent(i, b)
            send_near(b + 2)

        def one(n, _):
            to_slots(1 + 2 * (n // 2), n % 2, b)
            return 0

        lax.fori_loop(0, SIDE, one, 0)
        return 0

    lax.fori_loop(0, BLOCKS, near_block, 0)

    def total(s, t):
        o = prec(cc, t // 2, s, t % 2)
        group = lax.broadcasted_iota(jnp.int32, (GRP, 128), 0).astype(F32) + 1.0
        for src in range(LINE):
            member[:, src * 128 : src * 128 + 128] = to_bf16(group == tagbuf[src, pl.ds(o, 1), :])
        return jnp.dot(member[...], slots[o].reshape(LINE * BLOCKS * MOST, PTS), preferred_element_type=F32)

    def beside(step):
        return prec(cc, first, (second + step) % SIDE, cc)

    def served(n):
        return ((first + turn(n // 2)) % SIDE) * 2 + n % 2

    def far(n, _):
        t = served(n)
        whole = total((second + 2) % SIDE, t).astype(BF16)
        for half in range(2):
            dbuf[0, t, half] = whole[half * HALF : half * HALF + HALF]
            remote(dbuf.at[0, t, half], relay.at[half, t], d_sem, relay_sem.at[half, t], beside((1, 3)[half]))
        return 0

    lax.fori_loop(0, LINE, far, 0)

    def finish(t):
        whole = mine[t].reshape(2, HALF, PTS)
        for half in range(2):
            wait_bytes(sums.at[half, t], sums_sem.at[half, t])
            whole = whole + sums[half, t].astype(F32)
        done = (0.25 * whole).astype(BF16).reshape(GRP, PTS)
        here = t == first * 2 + cc

        @pl.when(here)
        def _():
            out[my_run] = done

        @pl.when(jnp.logical_not(here))
        def _():
            fbuf[t] = done
            remote(fbuf.at[t], out.at[my_run], f_sem, out_sem, prec(cc, t // 2, second, t % 2))

    def left(t):
        wait_bytes(dbuf.at[1:3, t], near_sem.at[t])

    def near(n, _):
        t = served(n)
        for half in range(2):
            whole = total((second + (1, 3)[half]) % SIDE, t)
            wait_bytes(relay.at[half, t], relay_sem.at[half, t])
            passed = whole[half * HALF : half * HALF + HALF] + relay[half, t].astype(F32)
            dbuf[1 + half, t, half] = passed.astype(BF16)
            dbuf[1 + half, t, 1 - half] = whole[(1 - half) * HALF : (1 - half) * HALF + HALF].astype(BF16)

        @pl.when(n >= 2)
        def _():
            left(served(n - 2))

        for half in range(2):
            remote(dbuf.at[1 + half, t], sums.at[half, t], near_sem.at[t], sums_sem.at[half, t], beside((1, 3)[half]))
        mine[t] = total(second, t)

        @pl.when(n >= BEHIND)
        def _():
            finish(served(n - BEHIND))

        return 0

    lax.fori_loop(0, LINE, near, 0)

    def last(n, _):
        finish(served(n))
        return 0

    lax.fori_loop(LINE - BEHIND, LINE, last, 0)
    left(served(LINE - 2))
    left(served(LINE - 1))

    wait_bytes(out.at[0 : RUNS - 1], out_sem)
    wait_bytes(fbuf.at[0 : LINE - 1], f_sem)
    wait_bytes(dbuf.at[0], d_sem)
    wait_bytes(infos.at[0 : LINE - 1], info_ssem)

    for b in range(BLOCKS):
        sent(3 - cc, b)
    for i in range(SIDE, RUNS):
        for b in (2, 3):
            sent(i, b)


def per_device(chromatograms, standards, library, owner_of, local_group, quality):
    vmem = pl.BlockSpec(memory_space=pltpu.VMEM)
    smem = pl.BlockSpec(memory_space=pltpu.SMEM)
    return pl.pallas_call(
        kernel,
        out_shape=pltpu.VMEM((RUNS, GRP, PTS), BF16),
        in_specs=[pl.BlockSpec(memory_space=pl.ANY), smem, smem, vmem, vmem, vmem],
        out_specs=vmem,
        scratch_shapes=[
            pltpu.VMEM((2, BLOCKS * BLOCK, PTS), BF16),
            pltpu.VMEM((BLOCK, BLOCK), BF16),
            pltpu.VMEM((BLOCKS * BLOCK, 128), F32),
            pltpu.VMEM((RUNS, 1, PTS), F32),
            pltpu.VMEM((2, 16, 128), jnp.int32),
            pltpu.VMEM((LINE, 2, 16, 128), jnp.int32),
            pltpu.VMEM((RUNS, BLOCKS, BLOCK, PTS), BF16),
            pltpu.VMEM((LINE, BLOCKS, BLOCK, PTS), BF16),
            pltpu.VMEM((OWNERS, LINE, BLOCKS, MOST, PTS), BF16),
            pltpu.VMEM((LINE, OWNERS, 128), F32),
            pltpu.VMEM((GRP, LINE * 128), BF16),
            pltpu.VMEM((3, LINE, 2, HALF, PTS), BF16),
            pltpu.VMEM((2, LINE, HALF, PTS), BF16),
            pltpu.VMEM((2, LINE, 2, HALF, PTS), BF16),
            pltpu.VMEM((LINE, GRP, PTS), F32),
            pltpu.VMEM((LINE, GRP, PTS), BF16),
            pltpu.SemaphoreType.DMA((2,)),
            pltpu.SemaphoreType.DMA,
            pltpu.SemaphoreType.DMA,
            pltpu.SemaphoreType.DMA((RUNS, BLOCKS)),
            pltpu.SemaphoreType.DMA((LINE, BLOCKS)),
            pltpu.SemaphoreType.DMA,
            pltpu.SemaphoreType.DMA((LINE,)),
            pltpu.SemaphoreType.DMA((2, LINE)),
            pltpu.SemaphoreType.DMA((2, LINE)),
            pltpu.SemaphoreType.DMA,
            pltpu.SemaphoreType.DMA,
        ],
        compiler_params=pltpu.CompilerParams(collective_id=0, has_side_effects=True, vmem_limit_bytes=58 * 2**20),
    )(
        chromatograms,
        standards,
        library,
        owner_of.reshape(16, 128),
        local_group.reshape(16, 128),
        quality.reshape(16, 128),
    )


def solution(mesh):
    placed = (P("run", "prec", None), P("run", None), P(), P("prec", None), P("prec"), P("prec"))
    return jax.shard_map(
        per_device, mesh=mesh, in_specs=placed, out_specs=P("run", "prec", None), check_vma=False
    )
```
